32 devices in a mesh: wide: 8 (over z, y), narrow: 4 (over x, core).
Axes of the slice: x: 2, y: 2, z: 4, core: 2. Of those that a mesh axis runs over, the one named last changes fastest.
Arguments:
- file_lengths: int32 [3], replicated, may hold values from 1 to 4, as said below
- queries: bfloat16 [4096, 4096], P('wide', 'narrow'), may hold values from -6 to 6
- out_grad: bfloat16 [4096, 4096], P('wide', 'narrow'), may hold values from -6 to 6
- mem_key: bfloat16 [1024, 1024], P('wide', 'narrow'), may hold values from -6 to 6
- memory_values: bfloat16 [1024, 1024], P('wide', 'narrow'), may hold values from -6 to 6
- enc_rows: bfloat16 [1024, 4096], P('wide'), may hold values from -6 to 6
- key_down: bfloat16 [4096, 128], replicated, may hold values from -0.09375 to 0.09375
- key_up: bfloat16 [128, 1024], P(None, 'narrow'), may hold values from -0.5 to 0.5
- value_down: bfloat16 [4096, 128], replicated, may hold values from -0.09375 to 0.09375
- value_up: bfloat16 [128, 1024], P(None, 'narrow'), may hold values from -0.5 to 0.5
Outputs:
- grad_key_down: float32 [4096, 128], P('wide')
- grad_value_down: float32 [4096, 128], P('wide')
- grad_key_up: float32 [128, 1024], P(None, 'narrow')
- grad_value_up: float32 [128, 1024], P(None, 'narrow')
The draws below stay inside these ranges and needn't reach their ends.
Inputs may be any that keep to these rules, and one draw needn't show every extreme that they name: `file_lengths`: the lengths sum to 8; the last file has 4 stretches.
All inputs are finite; a program needn't handle non-finite values.
Results may differ from the reference program's by a relative error of at most 0.0056.
Values may be sent and summed in bfloat16 or wider, within the bound.
A program may use at most 128 MiB of HBM per device.

```python
import jax
import jax.numpy as jnp
from jax import lax

D = 4096
HEAD_SIZE = 128
KEY_VALUE_HEADS = 8
Q_PER_KV = 4
LR = 128
QC = 512
MEMORY_ROWS = 128
STRETCH_TOTAL = 8
MAX_STRETCHES = 4
FILES = 3


def compose(key, total, parts, most):
    sizes = jnp.ones((parts,), jnp.int32)
    labels = jnp.arange(parts, dtype=jnp.int32)

    def step(turn, carry):
        current, state = carry
        state, sub = jax.random.split(state)
        score = jax.random.randint(sub, (parts,), 0, 1 << 20) * parts + labels
        score = jnp.where(current < most, score, -1)
        chosen = jnp.argmax(score).astype(jnp.int32)
        current = current + (labels == chosen).astype(jnp.int32)
        return (current, state)
    sizes, unused = lax.fori_loop(0, total - parts, step, (sizes, key))
    return sizes


def draw_file_lengths(key, part):
    most = MAX_STRETCHES
    before = STRETCH_TOTAL - most
    front = compose(jax.random.fold_in(key, 11), before, FILES - 1, most)
    return jnp.concatenate([front, jnp.full((1,), most, jnp.int32)], 0)


def with_spikes(result, stream_key, source, target, shards_of, factor):
    owner, partner = [(jnp.arange(result.shape[dim]) // (result.shape[dim] // shards_of)).reshape([-1 if axis == dim else 1 for axis in range(result.ndim)]) for dim in (source, target)]
    chosen = jax.random.permutation(stream_key, shards_of)[partner]
    strong = (owner == chosen) | (owner == (partner + shards_of // 2) % shards_of)
    return jnp.where(strong, factor * result, result)


def shard_levels(stream_key, shape, shards, least, high):
    def one(position, blocks):
        draws = jax.random.uniform(jax.random.fold_in(jax.random.fold_in(stream_key, 6), position), (blocks,), jnp.float32, least / len(shards), high / len(shards))
        return jnp.repeat(jnp.exp(draws), shape[position] // blocks).reshape((-1,) + (1,) * (len(shape) - position - 1))

    gain = one(*shards[0])
    for cut in shards[1:]:
        gain = gain * one(*cut)
    return gain


def scatter_about(own_key, shape, deviation, bound, cuts=(), kind=jnp.bfloat16):
    entries = deviation * jax.random.normal(own_key, shape, jnp.float32)
    if cuts:
        entries = entries * shard_levels(own_key, shape, cuts, -0.22, 0.18)
    return jnp.clip(entries, -bound, bound).astype(kind)


def gaussian_with(rng, extent, spread, most, shards, heavy, kind=jnp.bfloat16):
    result = spread * jax.random.normal(rng, extent, jnp.float32)
    if shards:
        result = result * shard_levels(rng, extent, shards, -0.22, 0.18)
    return jnp.clip(with_spikes(result, jax.random.fold_in(rng, 3), *heavy), -most, most).astype(kind)


def setup_inputs(seed: int = 0) -> dict:
    splits = jax.random.split(jax.random.key(seed), 11)
    file_lengths = draw_file_lengths(jax.random.fold_in(splits[10], 71), 0)
    queries = scatter_about(splits[1], (STRETCH_TOTAL * QC, KEY_VALUE_HEADS * Q_PER_KV * HEAD_SIZE), 1.0, 6.0, ((0, 8), (1, 4)))
    out_grad = scatter_about(splits[2], (STRETCH_TOTAL * QC, KEY_VALUE_HEADS * Q_PER_KV * HEAD_SIZE), 1.0, 6.0, ((0, 8), (1, 4)))
    mem_key = scatter_about(splits[3], (STRETCH_TOTAL * MEMORY_ROWS, KEY_VALUE_HEADS * HEAD_SIZE), 1.0, 6.0, ((0, 8), (1, 4)))
    memory_values = scatter_about(splits[4], (STRETCH_TOTAL * MEMORY_ROWS, KEY_VALUE_HEADS * HEAD_SIZE), 1.0, 6.0, ((0, 8), (1, 4)))
    enc_rows = gaussian_with(splits[5], (STRETCH_TOTAL * MEMORY_ROWS, D), 1.0, 6.0, ((0, 8),), (0, 1, 8, 2.0))
    key_down = scatter_about(splits[6], (D, LR), D ** -0.5, 0.09375)
    key_up = scatter_about(splits[7], (LR, KEY_VALUE_HEADS * HEAD_SIZE), LR ** -0.5, 0.5, ((1, 4),))
    value_down = scatter_about(splits[8], (D, LR), D ** -0.5, 0.09375)
    value_up = scatter_about(splits[9], (LR, KEY_VALUE_HEADS * HEAD_SIZE), LR ** -0.5, 0.5, ((1, 4),))
    return dict(file_lengths=file_lengths, queries=queries, out_grad=out_grad, mem_key=mem_key, memory_values=memory_values, enc_rows=enc_rows, key_down=key_down, key_up=key_up, value_down=value_down, value_up=value_up)


def stretch_grads(query, dout, keys, values, valid):
    scale = HEAD_SIZE ** -0.5
    qf = query.astype(jnp.float32)
    kf = keys.astype(jnp.float32)
    vf = values.astype(jnp.float32)
    df = dout.astype(jnp.float32)
    score = jnp.einsum('qgmd,kgd->gmqk', qf, kf) * scale
    mask = valid[None, None, None, :]
    expo = jnp.where(mask, jnp.exp(jnp.where(mask, score, 0.0)), 0.0)
    prob = expo / jnp.sum(expo, axis=-1, keepdims=True)
    prob_b = prob.astype(jnp.bfloat16).astype(jnp.float32)
    outp = jnp.einsum('gmqk,kgd->qgmd', prob_b, vf)
    delta = jnp.sum(df * outp, axis=-1)
    dprob = jnp.einsum('qgmd,kgd->gmqk', df, vf)
    dscore = (prob * (dprob - jnp.transpose(delta, (1, 2, 0))[..., None])).astype(jnp.bfloat16).astype(jnp.float32)
    dkey = jnp.einsum('gmqk,qgmd->kgd', dscore, qf) * scale
    dval = jnp.einsum('gmqk,qgmd->kgd', prob_b, df)
    return dkey, dval


def reference(file_lengths, queries, out_grad, mem_key, memory_values, enc_rows, key_down, key_up, value_down, value_up):
    key_value_width = KEY_VALUE_HEADS * HEAD_SIZE
    starts = jnp.cumsum(file_lengths).astype(jnp.int32) - file_lengths
    stretch_ids = jnp.arange(STRETCH_TOTAL, dtype=jnp.int32)
    first = jnp.max(jnp.where(starts[None, :] <= stretch_ids[:, None], starts[None, :], 0), axis=1)
    pos = stretch_ids - first
    qall = queries.reshape(STRETCH_TOTAL, QC, KEY_VALUE_HEADS, Q_PER_KV, HEAD_SIZE)
    dall = out_grad.reshape(STRETCH_TOTAL, QC, KEY_VALUE_HEADS, Q_PER_KV, HEAD_SIZE)
    kpad = jnp.concatenate([jnp.zeros(((MAX_STRETCHES - 1) * MEMORY_ROWS, key_value_width), jnp.bfloat16), mem_key], 0).reshape(STRETCH_TOTAL + MAX_STRETCHES - 1, MEMORY_ROWS, KEY_VALUE_HEADS, HEAD_SIZE)
    value_padded = jnp.concatenate([jnp.zeros(((MAX_STRETCHES - 1) * MEMORY_ROWS, key_value_width), jnp.bfloat16), memory_values], 0).reshape(STRETCH_TOTAL + MAX_STRETCHES - 1, MEMORY_ROWS, KEY_VALUE_HEADS, HEAD_SIZE)
    block_ids = jnp.arange(MAX_STRETCHES, dtype=jnp.int32)

    def one(column_index):
        kwin = lax.dynamic_slice_in_dim(kpad, column_index, MAX_STRETCHES, 0)[::-1].reshape(MAX_STRETCHES * MEMORY_ROWS, KEY_VALUE_HEADS, HEAD_SIZE)
        value_span_rows = lax.dynamic_slice_in_dim(value_padded, column_index, MAX_STRETCHES, 0)[::-1].reshape(MAX_STRETCHES * MEMORY_ROWS, KEY_VALUE_HEADS, HEAD_SIZE)
        valid = jnp.repeat(block_ids <= pos[column_index], MEMORY_ROWS)
        dkey, dval = stretch_grads(qall[column_index], dall[column_index], kwin, value_span_rows, valid)
        return dkey.reshape(MAX_STRETCHES, MEMORY_ROWS, key_value_width), dval.reshape(MAX_STRETCHES, MEMORY_ROWS, key_value_width)

    contrib_k, contrib_v = lax.map(one, stretch_ids)
    key_sum = jnp.zeros((STRETCH_TOTAL, MEMORY_ROWS, key_value_width), jnp.float32)
    val_sum = jnp.zeros((STRETCH_TOTAL, MEMORY_ROWS, key_value_width), jnp.float32)
    for j in range(MAX_STRETCHES):
        pad = jnp.zeros((j, MEMORY_ROWS, key_value_width), jnp.float32)
        key_sum = key_sum + jnp.concatenate([contrib_k[j:, j], pad], 0)
        val_sum = val_sum + jnp.concatenate([contrib_v[j:, j], pad], 0)
    key_grad = key_sum.reshape(STRETCH_TOTAL * MEMORY_ROWS, key_value_width).astype(jnp.bfloat16)
    value_grad = val_sum.reshape(STRETCH_TOTAL * MEMORY_ROWS, key_value_width).astype(jnp.bfloat16)
    u_key = jnp.dot(enc_rows, key_down, preferred_element_type=jnp.float32).astype(jnp.bfloat16)
    u_value = jnp.dot(enc_rows, value_down, preferred_element_type=jnp.float32).astype(jnp.bfloat16)
    h_key = jnp.dot(key_grad, key_up.T, preferred_element_type=jnp.float32).astype(jnp.bfloat16)
    h_value = jnp.dot(value_grad, value_up.T, preferred_element_type=jnp.float32).astype(jnp.bfloat16)
    grad_key_down = jnp.dot(enc_rows.T, h_key, preferred_element_type=jnp.float32)
    grad_value_down = jnp.dot(enc_rows.T, h_value, preferred_element_type=jnp.float32)
    grad_key_up = jnp.dot(u_key.T, key_grad, preferred_element_type=jnp.float32)
    grad_value_up = jnp.dot(u_value.T, value_grad, preferred_element_type=jnp.float32)
    return grad_key_down, grad_value_down, grad_key_up, grad_value_up
```

```python
import functools
import math

import jax
import jax.numpy as jnp
from jax import lax
from jax.experimental import pallas as pl
from jax.experimental.pallas import tpu as pltpu
from jax.sharding import PartitionSpec as P

HEAD_SIZE = 128
Q_PER_KV = 4
F32 = jnp.float32
BF16 = jnp.bfloat16
MESH = pl.DeviceIdType.MESH


def position_of(file_lengths, stretch):
    files = file_lengths.shape[0]
    start = jnp.int32(0)
    first = jnp.int32(0)
    for f in range(files):
        first = jnp.where(start <= stretch, start, first)
        start = start + file_lengths[f]
    return stretch - first


def passed_along(array, axis, by):
    devices = lax.axis_size(axis)
    pairs = [(i, i + by) for i in range(devices) if 0 <= i + by < devices]
    return lax.ppermute(array, axis, pairs)


def stretch_grads(query, dout, keys, values, valid):
    scale = HEAD_SIZE ** (-0.5)
    score = jnp.einsum("qgmd,kgd->gmqk", query, keys, preferred_element_type=F32) * scale
    mask = valid[None, None, None, :]
    expo = jnp.where(mask, jnp.exp(jnp.where(mask, score, 0.0)), 0.0)
    prob = expo / jnp.sum(expo, axis=-1, keepdims=True)
    prob_b = prob.astype(BF16)
    outp = jnp.einsum("gmqk,kgd->qgmd", prob_b, values, preferred_element_type=F32)
    delta = jnp.sum(dout.astype(F32) * outp, axis=-1)
    dprob = jnp.einsum("qgmd,kgd->gmqk", dout, values, preferred_element_type=F32)
    dscore = (prob * (dprob - jnp.transpose(delta, (1, 2, 0))[..., None])).astype(BF16)
    dkey = jnp.einsum("gmqk,qgmd->kgd", dscore, query, preferred_element_type=F32) * scale
    dval = jnp.einsum("gmqk,qgmd->kgd", prob_b, dout, preferred_element_type=F32)
    return (dkey, dval)


def by_collectives(file_lengths, queries, out_grad, mem_key, memory_values, enc_rows, key_down, key_up, value_down, value_up):
    wide_count = lax.axis_size("wide")
    span = min(8, wide_count // 2)
    rows, cols = mem_key.shape
    local_heads = cols // HEAD_SIZE
    stretch = lax.axis_index("wide")
    position = position_of(file_lengths, stretch)
    paired = jnp.stack([mem_key, memory_values])
    blocks = [paired]
    for offset in range(1, span):
        blocks.append(passed_along(paired, "wide", offset))
    window = jnp.stack(blocks)
    keys = window[:, 0].reshape(span * rows, local_heads, HEAD_SIZE)
    values = window[:, 1].reshape(span * rows, local_heads, HEAD_SIZE)
    valid = jnp.repeat(jnp.arange(span, dtype=jnp.int32) <= position, rows)
    query = queries.reshape(queries.shape[0], local_heads, Q_PER_KV, HEAD_SIZE)
    dout = out_grad.reshape(out_grad.shape[0], local_heads, Q_PER_KV, HEAD_SIZE)
    dkey, dval = stretch_grads(query, dout, keys, values, valid)
    contrib = jnp.stack([dkey.reshape(span, rows, cols), dval.reshape(span, rows, cols)], 1)
    total = contrib[0]
    for offset in range(1, span):
        total = total + passed_along(contrib[offset], "wide", -offset)
    key_grad = total[0].astype(BF16)
    value_grad = total[1].astype(BF16)
    u_key = jnp.dot(enc_rows, key_down, preferred_element_type=F32).astype(BF16)
    u_value = jnp.dot(enc_rows, value_down, preferred_element_type=F32).astype(BF16)
    part_key = jnp.dot(key_grad, key_up.T, preferred_element_type=F32)
    part_value = jnp.dot(value_grad, value_up.T, preferred_element_type=F32)
    h_key, h_value = lax.psum((part_key, part_value), "narrow")
    h_key = h_key.astype(BF16)
    h_value = h_value.astype(BF16)
    up_key = jnp.dot(u_key.T, key_grad, preferred_element_type=F32)
    up_value = jnp.dot(u_value.T, value_grad, preferred_element_type=F32)
    down_key = jnp.dot(enc_rows.T, h_key, preferred_element_type=F32)
    down_value = jnp.dot(enc_rows.T, h_value, preferred_element_type=F32)
    down_key, down_value, up_key, up_value = lax.psum((down_key, down_value, up_key, up_value), "wide")
    share = down_key.shape[0] // wide_count
    down_key = lax.dynamic_slice_in_dim(down_key, stretch * share, share, 0)
    down_value = lax.dynamic_slice_in_dim(down_value, stretch * share, share, 0)
    return (down_key, down_value, up_key, up_value)


NT = (((1,), (1,)), ((), ()))
TN = (((0,), (0,)), ((), ()))


def kernel(
    W, N, span,
    lengths, q_hbm, g_hbm, k_hbm, v_hbm, enc_hbm, kd_hbm, ku_hbm, vd_hbm, vu_hbm,
    okd, ovd, oku, ovu,
    q_v, g_v, kwin, vwin, enc_v, down_v, up_v,
    enc_slots, dk_acc, dv_acc, c_send, c_recv, u_v, kg_v,
    part32, part_send, part_recv, h_slots, rs_send, rs_recv, fin, res,
    local_sem, kv_s, kv_r, enc_s, enc_r, c_s, c_r, part_s, part_r, h_s, h_r, rs_s, rs_r, ag_s, ag_r, res_s, res_r,
):
    w = lax.axis_index("wide")
    n = lax.axis_index("narrow")
    half, kind = n // 2, n % 2
    rows, cols = k_hbm.shape
    groups = cols // HEAD_SIZE
    share = okd.shape[0]
    part_cols = share // 2
    rank = kd_hbm.shape[1]
    piece = rank // W
    scale = HEAD_SIZE ** (-0.5)

    def my_cols(owner):
        return pl.ds(pl.multiple_of(owner * share + half * part_cols, part_cols), part_cols)

    def local(i, src, dst):
        c = pltpu.make_async_copy(src, dst, local_sem.at[i])
        c.start()
        return c

    l_k = local(0, k_hbm, kwin.at[0])
    l_v = local(1, v_hbm, vwin.at[0])
    l_enc = local(2, enc_hbm, enc_v)
    l_kd = local(3, kd_hbm, down_v.at[:, pl.ds(0, rank)])
    l_vd = local(4, vd_hbm, down_v.at[:, pl.ds(rank, rank)])
    l_q = local(5, q_hbm, q_v)
    l_g = local(6, g_hbm, g_v)
    l_ku = local(7, ku_hbm, up_v.at[0])
    l_vu = local(8, vu_hbm, up_v.at[1])
    l_own = local(9, enc_hbm.at[:, my_cols(w)], enc_slots.at[0])

    barrier = pltpu.get_barrier_semaphore()
    for o in range(1, W):
        pl.semaphore_signal(barrier, inc=1, device_id=((w + o) % W, n), device_id_type=MESH)
    for o in range(1, N):
        pl.semaphore_signal(barrier, inc=1, device_id=(w, (n + o) % N), device_id_type=MESH)
    pl.semaphore_wait(barrier, W - 1 + N - 1)

    def remote(src, dst, ss, rs, to):
        return pltpu.make_async_remote_copy(
            src_ref=src, dst_ref=dst, send_sem=ss, recv_sem=rs, device_id=to, device_id_type=MESH
        )

    def kv_copy(j, t):
        src, dst = ((k_hbm, kwin), (v_hbm, vwin))[t]
        return remote(src, dst.at[j], kv_s.at[j, t], kv_r.at[j, t], ((w + j) % W, n))

    for j in range(1, span):
        @pl.when(w + j < W)
        def _():
            kv_copy(j, 0).start()
            kv_copy(j, 1).start()

        @pl.when(w < j)
        def _():
            kwin[j] = jnp.zeros((rows, cols), BF16)
            vwin[j] = jnp.zeros((rows, cols), BF16)

        @pl.when(w + j >= W)
        def _():
            for g in range(groups):
                c_recv[g, j] = jnp.zeros((2, rows, HEAD_SIZE), BF16)

    def enc_copy(o):
        to = (w + o) % W
        return remote(enc_hbm.at[:, my_cols(to)], enc_slots.at[o], enc_s.at[o], enc_r.at[o], (to, n))

    for o in range(1, W):
        enc_copy(o).start()

    l_enc.wait()
    l_kd.wait()
    l_vd.wait()
    u_v[...] = jnp.dot(enc_v[...], down_v[...], preferred_element_type=F32).astype(BF16)

    position = position_of(lengths, w)
    bias = [jnp.where(j <= position, 0.0, -1e30).astype(F32) for j in range(span)]
    l_k.wait()
    l_v.wait()
    l_q.wait()
    l_g.wait()
    for j in range(1, span):
        @pl.when(w >= j)
        def _():
            kv_copy(j, 0).wait_recv()
            kv_copy(j, 1).wait_recv()

    factor = scale * math.log2(math.e)
    chunk = 256
    n_chunks = q_v.shape[0] // chunk

    def c_copy(g, j):
        return remote(c_send.at[g, j], c_recv.at[g, j], c_s.at[g, j], c_r.at[g, j], ((w + W - j) % W, n))

    for g in range(groups):
        head_cols = slice(g * HEAD_SIZE, (g + 1) * HEAD_SIZE)
        dk_acc[g] = jnp.zeros((span * rows, HEAD_SIZE), F32)
        dv_acc[g] = jnp.zeros((span * rows, HEAD_SIZE), F32)

        def head(m, carry):
            col = pl.ds(pl.multiple_of((g * Q_PER_KV + m) * HEAD_SIZE, HEAD_SIZE), HEAD_SIZE)
            kg = kwin[:, :, head_cols].reshape(span * rows, HEAD_SIZE)
            vg = vwin[:, :, head_cols].reshape(span * rows, HEAD_SIZE)
            for c in range(n_chunks):
                qh = q_v[c * chunk:(c + 1) * chunk, col]
                dh = g_v[c * chunk:(c + 1) * chunk, col]
                s = lax.dot_general(kg, qh, NT, preferred_element_type=F32)
                dp = lax.dot_general(vg, dh, NT, preferred_element_type=F32)
                t = jnp.concatenate(
                    [s[j * rows:(j + 1) * rows] * factor + (bias[j] if j else 0.0) for j in range(span)], 0
                )
                e = jnp.exp2(t)
                r = 1.0 / jnp.sum(e, axis=0, keepdims=True)
                delta = jnp.sum(e * dp, axis=0, keepdims=True) * r
                p = e * r
                ds = (p * (dp - delta)).astype(BF16)
                dv_acc[g] += jnp.dot(p.astype(BF16), dh, preferred_element_type=F32)
                dk_acc[g] += jnp.dot(ds, qh, preferred_element_type=F32)
            return carry

        lax.fori_loop(0, Q_PER_KV, head, 0)
        for j in range(1, span):
            c_send[g, j, 0] = (dk_acc[g, j * rows:(j + 1) * rows] * scale).astype(BF16)
            c_send[g, j, 1] = dv_acc[g, j * rows:(j + 1) * rows].astype(BF16)

            @pl.when(w >= j)
            def _():
                c_copy(g, j).start()

    for g in range(groups):
        for j in range(1, span):
            @pl.when(w + j < W)
            def _():
                c_copy(g, j).wait_recv()

        key_total = dk_acc[g, :rows] * scale
        value_total = dv_acc[g, :rows]
        for j in range(1, span):
            key_total = key_total + c_recv[g, j, 0].astype(F32)
            value_total = value_total + c_recv[g, j, 1].astype(F32)
        kg_v[0, :, g * HEAD_SIZE:(g + 1) * HEAD_SIZE] = key_total.astype(BF16)
        kg_v[1, :, g * HEAD_SIZE:(g + 1) * HEAD_SIZE] = value_total.astype(BF16)

    l_ku.wait()
    l_vu.wait()
    for t in range(2):
        part = lax.dot_general(kg_v[t], up_v[t], NT, preferred_element_type=F32)
        part32[t] = part
        part_send[t] = part.astype(BF16)

    def part_copy(o):
        to = (n + o) % N
        return remote(part_send.at[to % 2], part_recv.at[o], part_s.at[o], part_r.at[o], (w, to))

    for o in range(1, N):
        part_copy(o).start()

    for t in range(2):
        up = lax.dot_general(u_v[:, t * rank:(t + 1) * rank], kg_v[t], TN, preferred_element_type=F32).astype(BF16)
        for i in range(W):
            rs_send[i, t] = up[i * piece:(i + 1) * piece]

    def rs_copy(o):
        to = (w + o) % W
        return remote(rs_send.at[to], rs_recv.at[o], rs_s.at[o], rs_r.at[o], (to, n))

    for o in range(1, W):
        rs_copy(o).start()

    total = part32[kind]
    for o in range(1, N):
        part_copy(o).wait_recv()
        total = total + part_recv[o].astype(F32)
    h_slots[0] = total.astype(BF16)

    def h_copy(o):
        return remote(h_slots.at[0], h_slots.at[o], h_s.at[o], h_r.at[o], ((w + o) % W, n))

    for o in range(1, W):
        h_copy(o).start()

    total = rs_send[w].astype(F32)
    for o in range(1, W):
        rs_copy(o).wait_recv()
        total = total + rs_recv[o].astype(F32)
    fin[w] = total.astype(BF16)

    def ag_copy(o, at):
        return remote(fin.at[w], fin.at[at], ag_s.at[o], ag_r.at[o], ((w + o) % W, n))

    for o in range(1, W):
        ag_copy(o, w).start()

    l_own.wait()
    for o in range(1, W):
        enc_copy(o).wait_recv()
        h_copy(o).wait_recv()
    down = lax.dot_general(
        enc_slots[...].reshape(W * rows, part_cols), h_slots[...].reshape(W * rows, rank), TN,
        preferred_element_type=F32,
    )
    res[n] = down.astype(BF16)

    def res_copy(o, at):
        return remote(res.at[n], res.at[at], res_s.at[o], res_r.at[o], (w, (n + o) % N))

    for o in range(1, N):
        res_copy(o, n).start()

    for o in range(1, W):
        ag_copy(o, (w + W - o) % W).wait_recv()
    for i in range(W):
        oku[i * piece:(i + 1) * piece, :] = fin[i, 0].astype(F32)
        ovu[i * piece:(i + 1) * piece, :] = fin[i, 1].astype(F32)
    for o in range(1, N):
        res_copy(o, (n + N - o) % N).wait_recv()
    for i in range(N):
        (okd, ovd)[i % 2][(i // 2) * part_cols:(i // 2 + 1) * part_cols, :] = res[i].astype(F32)

    for j in range(1, span):
        @pl.when(w + j < W)
        def _():
            kv_copy(j, 0).wait_send()
            kv_copy(j, 1).wait_send()

        @pl.when(w >= j)
        def _():
            for g in range(groups):
                c_copy(g, j).wait_send()
    for o in range(1, W):
        enc_copy(o).wait_send()
        rs_copy(o).wait_send()
        h_copy(o).wait_send()
        ag_copy(o, w).wait_send()
    for o in range(1, N):
        part_copy(o).wait_send()
        res_copy(o, n).wait_send()


def by_kernel(file_lengths, queries, out_grad, mem_key, memory_values, enc_rows, key_down, key_up, value_down, value_up):
    W, N = lax.axis_size("wide"), lax.axis_size("narrow")
    span = min(8, W // 2)
    rows, cols = mem_key.shape
    groups = cols // HEAD_SIZE
    width, rank = key_down.shape
    share = width // W
    half = share // 2
    piece = rank // W
    dma = pltpu.SemaphoreType.DMA
    any_spec = pl.BlockSpec(memory_space=pl.ANY)
    vmem_spec = pl.BlockSpec(memory_space=pltpu.VMEM)
    return pl.pallas_call(
        functools.partial(kernel, W, N, span),
        out_shape=(
            jax.ShapeDtypeStruct((share, rank), F32),
            jax.ShapeDtypeStruct((share, rank), F32),
            jax.ShapeDtypeStruct((rank, cols), F32),
            jax.ShapeDtypeStruct((rank, cols), F32),
        ),
        in_specs=[pl.BlockSpec(memory_space=pltpu.SMEM)] + [any_spec] * 9,
        out_specs=(vmem_spec,) * 4,
        scratch_shapes=[
            pltpu.VMEM(queries.shape, BF16),
            pltpu.VMEM(out_grad.shape, BF16),
            pltpu.VMEM((span, rows, cols), BF16),
            pltpu.VMEM((span, rows, cols), BF16),
            pltpu.VMEM((rows, width), BF16),
            pltpu.VMEM((width, 2 * rank), BF16),
            pltpu.VMEM((2, rank, cols), BF16),
            pltpu.VMEM((W, rows, half), BF16),
            pltpu.VMEM((groups, span * rows, HEAD_SIZE), F32),
            pltpu.VMEM((groups, span * rows, HEAD_SIZE), F32),
            pltpu.VMEM((groups, span, 2, rows, HEAD_SIZE), BF16),
            pltpu.VMEM((groups, span, 2, rows, HEAD_SIZE), BF16),
            pltpu.VMEM((rows, 2 * rank), BF16),
            pltpu.VMEM((2, rows, cols), BF16),
            pltpu.VMEM((2, rows, rank), F32),
            pltpu.VMEM((2, rows, rank), BF16),
            pltpu.VMEM((N, rows, rank), BF16),
            pltpu.VMEM((W, rows, rank), BF16),
            pltpu.VMEM((W, 2, piece, cols), BF16),
            pltpu.VMEM((W, 2, piece, cols), BF16),
            pltpu.VMEM((W, 2, piece, cols), BF16),
            pltpu.VMEM((N, half, rank), BF16),
            dma((10,)),
            dma((span, 2)), dma((span, 2)),
            dma((W,)), dma((W,)),
            dma((groups, span)), dma((groups, span)),
            dma((N,)), dma((N,)),
            dma((W,)), dma((W,)),
            dma((W,)), dma((W,)),
            dma((W,)), dma((W,)),
            dma((N,)), dma((N,)),
        ],
        compiler_params=pltpu.CompilerParams(
            collective_id=0, has_side_effects=True, vmem_limit_bytes=48 * 2**20
        ),
    )(file_lengths, queries, out_grad, mem_key, memory_values, enc_rows, key_down, key_up, value_down, value_up)


def solution(mesh):
    placed = (
        P(),
        P("wide", "narrow"),
        P("wide", "narrow"),
        P("wide", "narrow"),
        P("wide", "narrow"),
        P("wide", None),
        P(),
        P(None, "narrow"),
        P(),
        P(None, "narrow"),
    )

    def on_device(*args):
        W, N = lax.axis_size("wide"), lax.axis_size("narrow")
        width, rank = args[6].shape
        fits = N == 4 and width % (W * 256) == 0 and rank % (W * 16) == 0 and args[1].shape[0] % 256 == 0
        return (by_kernel if fits else by_collectives)(*args)

    return jax.shard_map(
        on_device,
        mesh=mesh,
        in_specs=placed,
        out_specs=(P("wide", None), P("wide", None), P(None, "narrow"), P(None, "narrow")),
        check_vma=False,
    )
```

```python
import functools
import math

import jax
import jax.numpy as jnp
from jax import lax
from jax.experimental import pallas as pl
from jax.experimental.pallas import tpu as pltpu
from jax.sharding import PartitionSpec as P

HEAD_SIZE = 128
Q_PER_KV = 4
F32 = jnp.float32
BF16 = jnp.bfloat16
MESH = pl.DeviceIdType.MESH


def position_of(file_lengths, stretch):
    files = file_lengths.shape[0]
    start = jnp.int32(0)
    first = jnp.int32(0)
    for f in range(files):
        first = jnp.where(start <= stretch, start, first)
        start = start + file_lengths[f]
    return stretch - first


def passed_along(array, axis, by):
    devices = lax.axis_size(axis)
    pairs = [(i, i + by) for i in range(devices) if 0 <= i + by < devices]
    return lax.ppermute(array, axis, pairs)


def stretch_grads(query, dout, keys, values, valid):
    scale = HEAD_SIZE ** (-0.5)
    score = jnp.einsum("qgmd,kgd->gmqk", query, keys, preferred_element_type=F32) * scale
    mask = valid[None, None, None, :]
    expo = jnp.where(mask, jnp.exp(jnp.where(mask, score, 0.0)), 0.0)
    prob = expo / jnp.sum(expo, axis=-1, keepdims=True)
    prob_b = prob.astype(BF16)
    outp = jnp.einsum("gmqk,kgd->qgmd", prob_b, values, preferred_element_type=F32)
    delta = jnp.sum(dout.astype(F32) * outp, axis=-1)
    dprob = jnp.einsum("qgmd,kgd->gmqk", dout, values, preferred_element_type=F32)
    dscore = (prob * (dprob - jnp.transpose(delta, (1, 2, 0))[..., None])).astype(BF16)
    dkey = jnp.einsum("gmqk,qgmd->kgd", dscore, query, preferred_element_type=F32) * scale
    dval = jnp.einsum("gmqk,qgmd->kgd", prob_b, dout, preferred_element_type=F32)
    return (dkey, dval)


def by_collectives(file_lengths, queries, out_grad, mem_key, memory_values, enc_rows, key_down, key_up, value_down, value_up):
    wide_count = lax.axis_size("wide")
    span = min(8, wide_count // 2)
    rows, cols = mem_key.shape
    local_heads = cols // HEAD_SIZE
    stretch = lax.axis_index("wide")
    position = position_of(file_lengths, stretch)
    paired = jnp.stack([mem_key, memory_values])
    blocks = [paired]
    for offset in range(1, span):
        blocks.append(passed_along(paired, "wide", offset))
    window = jnp.stack(blocks)
    keys = window[:, 0].reshape(span * rows, local_heads, HEAD_SIZE)
    values = window[:, 1].reshape(span * rows, local_heads, HEAD_SIZE)
    valid = jnp.repeat(jnp.arange(span, dtype=jnp.int32) <= position, rows)
    query = queries.reshape(queries.shape[0], local_heads, Q_PER_KV, HEAD_SIZE)
    dout = out_grad.reshape(out_grad.shape[0], local_heads, Q_PER_KV, HEAD_SIZE)
    dkey, dval = stretch_grads(query, dout, keys, values, valid)
    contrib = jnp.stack([dkey.reshape(span, rows, cols), dval.reshape(span, rows, cols)], 1)
    total = contrib[0]
    for offset in range(1, span):
        total = total + passed_along(contrib[offset], "wide", -offset)
    key_grad = total[0].astype(BF16)
    value_grad = total[1].astype(BF16)
    u_key = jnp.dot(enc_rows, key_down, preferred_element_type=F32).astype(BF16)
    u_value = jnp.dot(enc_rows, value_down, preferred_element_type=F32).astype(BF16)
    part_key = jnp.dot(key_grad, key_up.T, preferred_element_type=F32)
    part_value = jnp.dot(value_grad, value_up.T, preferred_element_type=F32)
    h_key, h_value = lax.psum((part_key, part_value), "narrow")
    h_key = h_key.astype(BF16)
    h_value = h_value.astype(BF16)
    up_key = jnp.dot(u_key.T, key_grad, preferred_element_type=F32)
    up_value = jnp.dot(u_value.T, value_grad, preferred_element_type=F32)
    down_key = jnp.dot(enc_rows.T, h_key, preferred_element_type=F32)
    down_value = jnp.dot(enc_rows.T, h_value, preferred_element_type=F32)
    down_key, down_value, up_key, up_value = lax.psum((down_key, down_value, up_key, up_value), "wide")
    share = down_key.shape[0] // wide_count
    down_key = lax.dynamic_slice_in_dim(down_key, stretch * share, share, 0)
    down_value = lax.dynamic_slice_in_dim(down_value, stretch * share, share, 0)
    return (down_key, down_value, up_key, up_value)


NT = (((1,), (1,)), ((), ()))
TN = (((0,), (0,)), ((), ()))


def kernel(
    W, N, span,
    lengths, q_hbm, g_hbm, k_hbm, v_hbm, enc_hbm, kd_hbm, ku_hbm, vd_hbm, vu_hbm,
    res, fin,
    q_v, g_v, kwin, vwin, enc_v, down_v, up_v,
    enc_slots, dk_acc, dv_acc, c_send, c_recv, u_v, kg_v,
    part32, part_send, part_recv, h_slots, rs_send, rs_recv,
    local_sem, kv_s, kv_r, enc_s, enc_r, c_s, c_r, part_s, part_r, h_s, h_r, rs_s, rs_r, ag_s, ag_r, res_s, res_r,
):
    w = lax.axis_index("wide")
    n = lax.axis_index("narrow")
    half, kind = n // 2, n % 2
    rows, cols = k_hbm.shape
    groups = cols // HEAD_SIZE
    part_cols = res.shape[1]
    share = 2 * part_cols
    rank = kd_hbm.shape[1]
    piece = rank // W
    scale = HEAD_SIZE ** (-0.5)

    def my_cols(owner):
        return pl.ds(pl.multiple_of(owner * share + half * part_cols, part_cols), part_cols)

    def local(i, src, dst):
        c = pltpu.make_async_copy(src, dst, local_sem.at[i])
        c.start()
        return c

    l_k = local(0, k_hbm, kwin.at[0])
    l_v = local(1, v_hbm, vwin.at[0])
    l_enc = local(2, enc_hbm, enc_v)
    l_kd = local(3, kd_hbm, down_v.at[:, pl.ds(0, rank)])
    l_vd = local(4, vd_hbm, down_v.at[:, pl.ds(rank, rank)])
    l_q = local(5, q_hbm, q_v)
    l_g = local(6, g_hbm, g_v)
    l_ku = local(7, ku_hbm, up_v.at[0])
    l_vu = local(8, vu_hbm, up_v.at[1])
    l_own = local(9, enc_hbm.at[:, my_cols(w)], enc_slots.at[0])

    barrier = pltpu.get_barrier_semaphore()
    for o in range(1, W):
        pl.semaphore_signal(barrier, inc=1, device_id=((w + o) % W, n), device_id_type=MESH)
    for o in range(1, N):
        pl.semaphore_signal(barrier, inc=1, device_id=(w, (n + o) % N), device_id_type=MESH)
    pl.semaphore_wait(barrier, W - 1 + N - 1)

    def remote(src, dst, ss, rs, to):
        return pltpu.make_async_remote_copy(
            src_ref=src, dst_ref=dst, send_sem=ss, recv_sem=rs, device_id=to, device_id_type=MESH
        )

    def kv_copy(j, t):
        src, dst = ((k_hbm, kwin), (v_hbm, vwin))[t]
        return remote(src, dst.at[j], kv_s.at[j, t], kv_r.at[j, t], ((w + j) % W, n))

    for j in range(1, span):
        @pl.when(w + j < W)
        def _():
            kv_copy(j, 0).start()
            kv_copy(j, 1).start()

        @pl.when(w < j)
        def _():
            kwin[j] = jnp.zeros((rows, cols), BF16)
            vwin[j] = jnp.zeros((rows, cols), BF16)

        @pl.when(w + j >= W)
        def _():
            for g in range(groups):
                c_recv[g, j] = jnp.zeros((2, rows, HEAD_SIZE), BF16)

    def enc_copy(o):
        to = (w + o) % W
        return remote(enc_hbm.at[:, my_cols(to)], enc_slots.at[o], enc_s.at[o], enc_r.at[o], (to, n))

    for o in range(1, W):
        enc_copy(o).start()

    l_enc.wait()
    l_kd.wait()
    l_vd.wait()
    u_v[...] = jnp.dot(enc_v[...], down_v[...], preferred_element_type=F32).astype(BF16)

    position = position_of(lengths, w)
    bias = [jnp.where(j <= position, 0.0, -1e30).astype(F32) for j in range(span)]
    l_k.wait()
    l_v.wait()
    l_q.wait()
    l_g.wait()
    for j in range(1, span):
        @pl.when(w >= j)
        def _():
            kv_copy(j, 0).wait_recv()
            kv_copy(j, 1).wait_recv()
    factor = scale * math.log2(math.e)
    chunk = 256
    n_chunks = q_v.shape[0] // chunk

    def c_copy(g, j):
        return remote(c_send.at[g, j], c_recv.at[g, j], c_s.at[g, j], c_r.at[g, j], ((w + W - j) % W, n))

    for g in range(groups):
        head_cols = slice(g * HEAD_SIZE, (g + 1) * HEAD_SIZE)
        dk_acc[g] = jnp.zeros((span * rows, HEAD_SIZE), F32)
        dv_acc[g] = jnp.zeros((span * rows, HEAD_SIZE), F32)

        def head(m, carry):
            col = pl.ds(pl.multiple_of((g * Q_PER_KV + m) * HEAD_SIZE, HEAD_SIZE), HEAD_SIZE)
            kg = kwin[:, :, head_cols].reshape(span * rows, HEAD_SIZE)
            vg = vwin[:, :, head_cols].reshape(span * rows, HEAD_SIZE)
            for c in range(n_chunks):
                qh = q_v[c * chunk:(c + 1) * chunk, col]
                dh = g_v[c * chunk:(c + 1) * chunk, col]
                s = lax.dot_general(kg, qh, NT, preferred_element_type=F32)
                dp = lax.dot_general(vg, dh, NT, preferred_element_type=F32)
                t = jnp.concatenate(
                    [s[j * rows:(j + 1) * rows] * factor + (bias[j] if j else 0.0) for j in range(span)], 0
                )
                e = jnp.exp2(t)
                r = 1.0 / jnp.sum(e, axis=0, keepdims=True)
                delta = jnp.sum(e * dp, axis=0, keepdims=True) * r
                p = e * r
                ds = (p * (dp - delta)).astype(BF16)
                dv_acc[g] += jnp.dot(p.astype(BF16), dh, preferred_element_type=F32)
                dk_acc[g] += jnp.dot(ds, qh, preferred_element_type=F32)
            return carry

        lax.fori_loop(0, Q_PER_KV, head, 0)
        for j in range(1, span):
            c_send[g, j, 0] = (dk_acc[g, j * rows:(j + 1) * rows] * scale).astype(BF16)
            c_send[g, j, 1] = dv_acc[g, j * rows:(j + 1) * rows].astype(BF16)

            @pl.when(w >= j)
            def _():
                c_copy(g, j).start()

    for g in range(groups):
        for j in range(1, span):
            @pl.when(w + j < W)
            def _():
                c_copy(g, j).wait_recv()

        key_total = dk_acc[g, :rows] * scale
        value_total = dv_acc[g, :rows]
        for j in range(1, span):
            key_total = key_total + c_recv[g, j, 0].astype(F32)
            value_total = value_total + c_recv[g, j, 1].astype(F32)
        kg_v[0, :, g * HEAD_SIZE:(g + 1) * HEAD_SIZE] = key_total.astype(BF16)
        kg_v[1, :, g * HEAD_SIZE:(g + 1) * HEAD_SIZE] = value_total.astype(BF16)

    l_ku.wait()
    l_vu.wait()
    for t in range(2):
        part = lax.dot_general(kg_v[t], up_v[t], NT, preferred_element_type=F32)
        part32[t] = part
        part_send[t] = part.astype(BF16)

    def part_copy(o):
        to = (n + o) % N
        return remote(part_send.at[to % 2], part_recv.at[o], part_s.at[o], part_r.at[o], (w, to))

    for o in range(1, N):
        part_copy(o).start()

    for t in range(2):
        up = lax.dot_general(u_v[:, t * rank:(t + 1) * rank], kg_v[t], TN, preferred_element_type=F32).astype(BF16)
        for i in range(W):
            rs_send[i, t] = up[i * piece:(i + 1) * piece]

    def rs_copy(o):
        to = (w + o) % W
        return remote(rs_send.at[to], rs_recv.at[o], rs_s.at[o], rs_r.at[o], (to, n))

    for o in range(1, W):
        rs_copy(o).start()

    total = part32[kind]
    for o in range(1, N):
        part_copy(o).wait_recv()
        total = total + part_recv[o].astype(F32)
    h_slots[0] = total.astype(BF16)

    def h_copy(o):
        return remote(h_slots.at[0], h_slots.at[o], h_s.at[o], h_r.at[o], ((w + o) % W, n))

    for o in range(1, W):
        h_copy(o).start()

    total = rs_send[w].astype(F32)
    for o in range(1, W):
        rs_copy(o).wait_recv()
        total = total + rs_recv[o].astype(F32)
    fin[w] = total.astype(BF16)

    def ag_copy(o, at):
        return remote(fin.at[w], fin.at[at], ag_s.at[o], ag_r.at[o], ((w + o) % W, n))

    for o in range(1, W):
        ag_copy(o, w).start()

    l_own.wait()
    for o in range(1, W):
        enc_copy(o).wait_recv()
        h_copy(o).wait_recv()
    down = lax.dot_general(
        enc_slots[...].reshape(W * rows, part_cols), h_slots[...].reshape(W * rows, rank), TN,
        preferred_element_type=F32,
    )
    res[n] = down.astype(BF16)

    def res_copy(o, at):
        return remote(res.at[n], res.at[at], res_s.at[o], res_r.at[o], (w, (n + o) % N))

    for o in range(1, N):
        res_copy(o, n).start()

    for o in range(1, W):
        ag_copy(o, (w + W - o) % W).wait_recv()
    for o in range(1, N):
        res_copy(o, (n + N - o) % N).wait_recv()

    for j in range(1, span):
        @pl.when(w + j < W)
        def _():
            kv_copy(j, 0).wait_send()
            kv_copy(j, 1).wait_send()

        @pl.when(w >= j)
        def _():
            for g in range(groups):
                c_copy(g, j).wait_send()
    for o in range(1, W):
        enc_copy(o).wait_send()
        rs_copy(o).wait_send()
        h_copy(o).wait_send()
        ag_copy(o, w).wait_send()
    for o in range(1, N):
        part_copy(o).wait_send()
        res_copy(o, n).wait_send()


def widen(res, fin, okd, ovd, oku, ovu):
    part_cols = res.shape[1]
    piece = fin.shape[2]
    for i in range(fin.shape[0]):
        oku[i * piece:(i + 1) * piece, :] = fin[i, 0].astype(F32)
        ovu[i * piece:(i + 1) * piece, :] = fin[i, 1].astype(F32)
    for i in range(res.shape[0]):
        (okd, ovd)[i % 2][(i // 2) * part_cols:(i // 2 + 1) * part_cols, :] = res[i].astype(F32)


def by_kernel(file_lengths, queries, out_grad, mem_key, memory_values, enc_rows, key_down, key_up, value_down, value_up):
    W, N = lax.axis_size("wide"), lax.axis_size("narrow")
    span = min(8, W // 2)
    rows, cols = mem_key.shape
    groups = cols // HEAD_SIZE
    width, rank = key_down.shape
    share = width // W
    half = share // 2
    piece = rank // W
    dma = pltpu.SemaphoreType.DMA
    any_spec = pl.BlockSpec(memory_space=pltpu.HBM)
    vmem_spec = pl.BlockSpec(memory_space=pltpu.VMEM)
    res, fin = pl.pallas_call(
        functools.partial(kernel, W, N, span),
        out_shape=(
            jax.ShapeDtypeStruct((N, half, rank), BF16),
            jax.ShapeDtypeStruct((W, 2, piece, cols), BF16),
        ),
        in_specs=[pl.BlockSpec(memory_space=pltpu.SMEM)] + [any_spec] * 9,
        out_specs=(vmem_spec,) * 2,
        scratch_shapes=[
            pltpu.VMEM(queries.shape, BF16),
            pltpu.VMEM(out_grad.shape, BF16),
            pltpu.VMEM((span, rows, cols), BF16),
            pltpu.VMEM((span, rows, cols), BF16),
            pltpu.VMEM((rows, width), BF16),
            pltpu.VMEM((width, 2 * rank), BF16),
            pltpu.VMEM((2, rank, cols), BF16),
            pltpu.VMEM((W, rows, half), BF16),
            pltpu.VMEM((groups, span * rows, HEAD_SIZE), F32),
            pltpu.VMEM((groups, span * rows, HEAD_SIZE), F32),
            pltpu.VMEM((groups, span, 2, rows, HEAD_SIZE), BF16),
            pltpu.VMEM((groups, span, 2, rows, HEAD_SIZE), BF16),
            pltpu.VMEM((rows, 2 * rank), BF16),
            pltpu.VMEM((2, rows, cols), BF16),
            pltpu.VMEM((2, rows, rank), F32),
            pltpu.VMEM((2, rows, rank), BF16),
            pltpu.VMEM((N, rows, rank), BF16),
            pltpu.VMEM((W, rows, rank), BF16),
            pltpu.VMEM((W, 2, piece, cols), BF16),
            pltpu.VMEM((W, 2, piece, cols), BF16),
            dma((10,)),
            dma((span, 2)), dma((span, 2)),
            dma((W,)), dma((W,)),
            dma((groups, span)), dma((groups, span)),
            dma((N,)), dma((N,)),
            dma((W,)), dma((W,)),
            dma((W,)), dma((W,)),
            dma((W,)), dma((W,)),
            dma((N,)), dma((N,)),
        ],
        compiler_params=pltpu.CompilerParams(
            collective_id=0, has_side_effects=True, vmem_limit_bytes=60 * 2**20
        ),
    )(file_lengths, queries, out_grad, mem_key, memory_values, enc_rows, key_down, key_up, value_down, value_up)
    return pl.pallas_call(
        widen,
        out_shape=(
            jax.ShapeDtypeStruct((share, rank), F32),
            jax.ShapeDtypeStruct((share, rank), F32),
            jax.ShapeDtypeStruct((rank, cols), F32),
            jax.ShapeDtypeStruct((rank, cols), F32),
        ),
        in_specs=[vmem_spec] * 2,
        out_specs=(vmem_spec,) * 4,
    )(res, fin)


def solution(mesh):
    placed = (
        P(),
        P("wide", "narrow"),
        P("wide", "narrow"),
        P("wide", "narrow"),
        P("wide", "narrow"),
        P("wide", None),
        P(),
        P(None, "narrow"),
        P(),
        P(None, "narrow"),
    )

    def on_device(*args):
        W, N = lax.axis_size("wide"), lax.axis_size("narrow")
        width, rank = args[6].shape
        fits = N == 4 and width % (W * 256) == 0 and rank % (W * 16) == 0 and args[1].shape[0] % 256 == 0
        return (by_kernel if fits else by_collectives)(*args)

    return jax.shard_map(
        on_device,
        mesh=mesh,
        in_specs=placed,
        out_specs=(P("wide", None), P("wide", None), P(None, "narrow"), P(None, "narrow")),
        check_vma=False,
    )
```

```python
import functools
import math

import jax
import jax.numpy as jnp
from jax import lax
from jax.experimental import pallas as pl
from jax.experimental.pallas import tpu as pltpu
from jax.sharding import PartitionSpec as P

HEAD_SIZE = 128
Q_PER_KV = 4
F32 = jnp.float32
BF16 = jnp.bfloat16
MESH = pl.DeviceIdType.MESH


def position_of(file_lengths, stretch):
    files = file_lengths.shape[0]
    start = jnp.int32(0)
    first = jnp.int32(0)
    for f in range(files):
        first = jnp.where(start <= stretch, start, first)
        start = start + file_lengths[f]
    return stretch - first


def passed_along(array, axis, by):
    devices = lax.axis_size(axis)
    pairs = [(i, i + by) for i in range(devices) if 0 <= i + by < devices]
    return lax.ppermute(array, axis, pairs)


def stretch_grads(query, dout, keys, values, valid):
    scale = HEAD_SIZE ** (-0.5)
    score = jnp.einsum("qgmd,kgd->gmqk", query, keys, preferred_element_type=F32) * scale
    mask = valid[None, None, None, :]
    expo = jnp.where(mask, jnp.exp(jnp.where(mask, score, 0.0)), 0.0)
    prob = expo / jnp.sum(expo, axis=-1, keepdims=True)
    prob_b = prob.astype(BF16)
    outp = jnp.einsum("gmqk,kgd->qgmd", prob_b, values, preferred_element_type=F32)
    delta = jnp.sum(dout.astype(F32) * outp, axis=-1)
    dprob = jnp.einsum("qgmd,kgd->gmqk", dout, values, preferred_element_type=F32)
    dscore = (prob * (dprob - jnp.transpose(delta, (1, 2, 0))[..., None])).astype(BF16)
    dkey = jnp.einsum("gmqk,qgmd->kgd", dscore, query, preferred_element_type=F32) * scale
    dval = jnp.einsum("gmqk,qgmd->kgd", prob_b, dout, preferred_element_type=F32)
    return (dkey, dval)


def by_collectives(file_lengths, queries, out_grad, mem_key, memory_values, enc_rows, key_down, key_up, value_down, value_up):
    wide_count = lax.axis_size("wide")
    span = min(8, wide_count // 2)
    rows, cols = mem_key.shape
    local_heads = cols // HEAD_SIZE
    stretch = lax.axis_index("wide")
    position = position_of(file_lengths, stretch)
    paired = jnp.stack([mem_key, memory_values])
    blocks = [paired]
    for offset in range(1, span):
        blocks.append(passed_along(paired, "wide", offset))
    window = jnp.stack(blocks)
    keys = window[:, 0].reshape(span * rows, local_heads, HEAD_SIZE)
    values = window[:, 1].reshape(span * rows, local_heads, HEAD_SIZE)
    valid = jnp.repeat(jnp.arange(span, dtype=jnp.int32) <= position, rows)
    query = queries.reshape(queries.shape[0], local_heads, Q_PER_KV, HEAD_SIZE)
    dout = out_grad.reshape(out_grad.shape[0], local_heads, Q_PER_KV, HEAD_SIZE)
    dkey, dval = stretch_grads(query, dout, keys, values, valid)
    contrib = jnp.stack([dkey.reshape(span, rows, cols), dval.reshape(span, rows, cols)], 1)
    total = contrib[0]
    for offset in range(1, span):
        total = total + passed_along(contrib[offset], "wide", -offset)
    key_grad = total[0].astype(BF16)
    value_grad = total[1].astype(BF16)
    u_key = jnp.dot(enc_rows, key_down, preferred_element_type=F32).astype(BF16)
    u_value = jnp.dot(enc_rows, value_down, preferred_element_type=F32).astype(BF16)
    part_key = jnp.dot(key_grad, key_up.T, preferred_element_type=F32)
    part_value = jnp.dot(value_grad, value_up.T, preferred_element_type=F32)
    h_key, h_value = lax.psum((part_key, part_value), "narrow")
    h_key = h_key.astype(BF16)
    h_value = h_value.astype(BF16)
    up_key = jnp.dot(u_key.T, key_grad, preferred_element_type=F32)
    up_value = jnp.dot(u_value.T, value_grad, preferred_element_type=F32)
    down_key = jnp.dot(enc_rows.T, h_key, preferred_element_type=F32)
    down_value = jnp.dot(enc_rows.T, h_value, preferred_element_type=F32)
    down_key, down_value, up_key, up_value = lax.psum((down_key, down_value, up_key, up_value), "wide")
    share = down_key.shape[0] // wide_count
    down_key = lax.dynamic_slice_in_dim(down_key, stretch * share, share, 0)
    down_value = lax.dynamic_slice_in_dim(down_value, stretch * share, share, 0)
    return (down_key, down_value, up_key, up_value)


NT = (((1,), (1,)), ((), ()))
TN = (((0,), (0,)), ((), ()))


def kernel(
    W, N, span,
    lengths, q_hbm, g_hbm, k_hbm, v_hbm, enc_hbm, kd_hbm, ku_hbm, vd_hbm, vu_hbm,
    res, fin,
    q_v, g_v, kwin, vwin, enc_v, down_v, up_v,
    enc_slots, dk_acc, dv_acc, c_send, c_recv, u_v, kg_v,
    part32, part_send, part_recv, h_slots, rs_send, rs_recv,
    local_sem, kv_s, kv_r, enc_s, enc_r, c_s, c_r, part_s, part_r, h_s, h_r, rs_s, rs_r, ag_s, ag_r, res_s, res_r,
):
    w = lax.axis_index("wide")
    n = lax.axis_index("narrow")
    half, kind = n // 2, n % 2
    rows, cols = k_hbm.shape
    groups = cols // HEAD_SIZE
    part_cols = res.shape[1]
    share = 2 * part_cols
    rank = kd_hbm.shape[1]
    piece = rank // W
    scale = HEAD_SIZE ** (-0.5)

    def my_cols(owner):
        return pl.ds(pl.multiple_of(owner * share + half * part_cols, part_cols), part_cols)

    def local(i, src, dst):
        c = pltpu.make_async_copy(src, dst, local_sem.at[i])
        c.start()
        return c

    l_k = local(0, k_hbm, kwin.at[0])
    l_v = local(1, v_hbm, vwin.at[0])
    l_enc = local(2, enc_hbm, enc_v)
    l_kd = local(3, kd_hbm, down_v.at[:, pl.ds(0, rank)])
    l_vd = local(4, vd_hbm, down_v.at[:, pl.ds(rank, rank)])
    l_q = local(5, q_hbm, q_v)
    l_g = local(6, g_hbm, g_v)
    l_ku = local(7, ku_hbm, up_v.at[0])
    l_vu = local(8, vu_hbm, up_v.at[1])
    l_own = local(9, enc_hbm.at[:, my_cols(w)], enc_slots.at[0])

    barrier = pltpu.get_barrier_semaphore()
    for o in range(1, W):
        pl.semaphore_signal(barrier, inc=1, device_id=((w + o) % W, n), device_id_type=MESH)
    for o in range(1, N):
        pl.semaphore_signal(barrier, inc=1, device_id=(w, (n + o) % N), device_id_type=MESH)
    pl.semaphore_wait(barrier, W - 1 + N - 1)

    def remote(src, dst, ss, rs, to):
        return pltpu.make_async_remote_copy(
            src_ref=src, dst_ref=dst, send_sem=ss, recv_sem=rs, device_id=to, device_id_type=MESH
        )

    def kv_copy(j, t):
        src, dst = ((k_hbm, kwin), (v_hbm, vwin))[t]
        return remote(src, dst.at[j], kv_s.at[j, t], kv_r.at[j, t], ((w + j) % W, n))

    for j in range(1, span):
        @pl.when(w + j < W)
        def _():
            kv_copy(j, 0).start()
            kv_copy(j, 1).start()

        @pl.when(w < j)
        def _():
            kwin[j] = jnp.zeros((rows, cols), BF16)
            vwin[j] = jnp.zeros((rows, cols), BF16)

        @pl.when(w + j >= W)
        def _():
            for g in range(groups):
                c_recv[g, j] = jnp.zeros((2, rows, HEAD_SIZE), BF16)

    def enc_copy(o):
        to = (w + o) % W
        return remote(enc_hbm.at[:, my_cols(to)], enc_slots.at[o], enc_s.at[o], enc_r.at[o], (to, n))

    for o in range(1, W):
        enc_copy(o).start()

    position = position_of(lengths, w)
    bias = [jnp.where(j <= position, 0.0, -1e30).astype(F32) for j in range(span)]
    l_k.wait()
    l_v.wait()
    l_q.wait()
    l_g.wait()
    for j in range(1, span):
        @pl.when(w >= j)
        def _():
            kv_copy(j, 0).wait_recv()
            kv_copy(j, 1).wait_recv()
    factor = scale * math.log2(math.e)
    chunk = 512
    n_chunks = q_v.shape[0] // chunk

    def c_copy(g, j):
        return remote(c_send.at[g, j], c_recv.at[g, j], c_s.at[g, j], c_r.at[g, j], ((w + W - j) % W, n))

    for g in range(groups):
        head_cols = slice(g * HEAD_SIZE, (g + 1) * HEAD_SIZE)
        dk_acc[g] = jnp.zeros((span * rows, HEAD_SIZE), F32)
        dv_acc[g] = jnp.zeros((span * rows, HEAD_SIZE), F32)

        def head(m, carry):
            col = pl.ds(pl.multiple_of((g * Q_PER_KV + m) * HEAD_SIZE, HEAD_SIZE), HEAD_SIZE)
            kg = kwin[:, :, head_cols].reshape(span * rows, HEAD_SIZE)
            vg = vwin[:, :, head_cols].reshape(span * rows, HEAD_SIZE)
            for c in range(n_chunks):
                qh = q_v[c * chunk:(c + 1) * chunk, col]
                dh = g_v[c * chunk:(c + 1) * chunk, col]
                s = lax.dot_general(kg, qh, NT, preferred_element_type=F32)
                dp = lax.dot_general(vg, dh, NT, preferred_element_type=F32)
                t = jnp.concatenate(
                    [s[j * rows:(j + 1) * rows] * factor + (bias[j] if j else 0.0) for j in range(span)], 0
                )
                e = jnp.exp2(t)
                r = 1.0 / jnp.sum(e, axis=0, keepdims=True)
                delta = jnp.sum(e * dp, axis=0, keepdims=True) * r
                p = e * r
                ds = (p * (dp - delta)).astype(BF16)
                dv_acc[g] += jnp.dot(p.astype(BF16), dh, preferred_element_type=F32)
                dk_acc[g] += jnp.dot(ds, qh, preferred_element_type=F32)
            return carry

        lax.fori_loop(0, Q_PER_KV, head, 0)
        for j in range(1, span):
            c_send[g, j, 0] = (dk_acc[g, j * rows:(j + 1) * rows] * scale).astype(BF16)
            c_send[g, j, 1] = dv_acc[g, j * rows:(j + 1) * rows].astype(BF16)

            @pl.when(w >= j)
            def _():
                c_copy(g, j).start()

    l_enc.wait()
    l_kd.wait()
    l_vd.wait()
    u_v[...] = jnp.dot(enc_v[...], down_v[...], preferred_element_type=F32).astype(BF16)

    for g in range(groups):
        for j in range(1, span):
            @pl.when(w + j < W)
            def _():
                c_copy(g, j).wait_recv()

        key_total = dk_acc[g, :rows] * scale
        value_total = dv_acc[g, :rows]
        for j in range(1, span):
            key_total = key_total + c_recv[g, j, 0].astype(F32)
            value_total = value_total + c_recv[g, j, 1].astype(F32)
        kg_v[0, :, g * HEAD_SIZE:(g + 1) * HEAD_SIZE] = key_total.astype(BF16)
        kg_v[1, :, g * HEAD_SIZE:(g + 1) * HEAD_SIZE] = value_total.astype(BF16)

    l_ku.wait()
    l_vu.wait()
    for t in range(2):
        part = lax.dot_general(kg_v[t], up_v[t], NT, preferred_element_type=F32)
        part32[t] = part
        part_send[t] = part.astype(BF16)

    def part_copy(o):
        to = (n + o) % N
        return remote(part_send.at[to % 2], part_recv.at[o], part_s.at[o], part_r.at[o], (w, to))

    for o in range(1, N):
        part_copy(o).start()

    for t in range(2):
        up = lax.dot_general(u_v[:, t * rank:(t + 1) * rank], kg_v[t], TN, preferred_element_type=F32).astype(BF16)
        for i in range(W):
            rs_send[i, t] = up[i * piece:(i + 1) * piece]

    def rs_copy(o):
        to = (w + o) % W
        return remote(rs_send.at[to], rs_recv.at[o], rs_s.at[o], rs_r.at[o], (to, n))

    for o in range(1, W):
        rs_copy(o).start()

    total = part32[kind]
    for o in range(1, N):
        part_copy(o).wait_recv()
        total = total + part_recv[o].astype(F32)
    h_slots[0] = total.astype(BF16)

    def h_copy(o):
        return remote(h_slots.at[0], h_slots.at[o], h_s.at[o], h_r.at[o], ((w + o) % W, n))

    for o in range(1, W):
        h_copy(o).start()

    total = rs_send[w].astype(F32)
    for o in range(1, W):
        rs_copy(o).wait_recv()
        total = total + rs_recv[o].astype(F32)
    fin[w] = total.astype(BF16)

    def ag_copy(o, at):
        return remote(fin.at[w], fin.at[at], ag_s.at[o], ag_r.at[o], ((w + o) % W, n))

    for o in range(1, W):
        ag_copy(o, w).start()

    l_own.wait()
    for o in range(1, W):
        enc_copy(o).wait_recv()
        h_copy(o).wait_recv()
    down = lax.dot_general(
        enc_slots[...].reshape(W * rows, part_cols), h_slots[...].reshape(W * rows, rank), TN,
        preferred_element_type=F32,
    )
    res[n] = down.astype(BF16)

    def res_copy(o, at):
        return remote(res.at[n], res.at[at], res_s.at[o], res_r.at[o], (w, (n + o) % N))

    for o in range(1, N):
        res_copy(o, n).start()

    for o in range(1, W):
        ag_copy(o, (w + W - o) % W).wait_recv()
    for o in range(1, N):
        res_copy(o, (n + N - o) % N).wait_recv()

    for j in range(1, span):
        @pl.when(w + j < W)
        def _():
            kv_copy(j, 0).wait_send()
            kv_copy(j, 1).wait_send()

        @pl.when(w >= j)
        def _():
            for g in range(groups):
                c_copy(g, j).wait_send()
    for o in range(1, W):
        enc_copy(o).wait_send()
        rs_copy(o).wait_send()
        h_copy(o).wait_send()
        ag_copy(o, w).wait_send()
    for o in range(1, N):
        part_copy(o).wait_send()
        res_copy(o, n).wait_send()


def widen(res, fin, okd, ovd, oku, ovu):
    part_cols = res.shape[1]
    piece = fin.shape[2]
    for i in range(fin.shape[0]):
        oku[i * piece:(i + 1) * piece, :] = fin[i, 0].astype(F32)
        ovu[i * piece:(i + 1) * piece, :] = fin[i, 1].astype(F32)
    for i in range(res.shape[0]):
        (okd, ovd)[i % 2][(i // 2) * part_cols:(i // 2 + 1) * part_cols, :] = res[i].astype(F32)


def by_kernel(file_lengths, queries, out_grad, mem_key, memory_values, enc_rows, key_down, key_up, value_down, value_up):
    W, N = lax.axis_size("wide"), lax.axis_size("narrow")
    span = min(8, W // 2)
    rows, cols = mem_key.shape
    groups = cols // HEAD_SIZE
    width, rank = key_down.shape
    share = width // W
    half = share // 2
    piece = rank // W
    dma = pltpu.SemaphoreType.DMA
    any_spec = pl.BlockSpec(memory_space=pltpu.HBM)
    vmem_spec = pl.BlockSpec(memory_space=pltpu.VMEM)
    res, fin = pl.pallas_call(
        functools.partial(kernel, W, N, span),
        out_shape=(
            jax.ShapeDtypeStruct((N, half, rank), BF16),
            jax.ShapeDtypeStruct((W, 2, piece, cols), BF16),
        ),
        in_specs=[pl.BlockSpec(memory_space=pltpu.SMEM)] + [any_spec] * 9,
        out_specs=(vmem_spec,) * 2,
        scratch_shapes=[
            pltpu.VMEM(queries.shape, BF16),
            pltpu.VMEM(out_grad.shape, BF16),
            pltpu.VMEM((span, rows, cols), BF16),
            pltpu.VMEM((span, rows, cols), BF16),
            pltpu.VMEM((rows, width), BF16),
            pltpu.VMEM((width, 2 * rank), BF16),
            pltpu.VMEM((2, rank, cols), BF16),
            pltpu.VMEM((W, rows, half), BF16),
            pltpu.VMEM((groups, span * rows, HEAD_SIZE), F32),
            pltpu.VMEM((groups, span * rows, HEAD_SIZE), F32),
            pltpu.VMEM((groups, span, 2, rows, HEAD_SIZE), BF16),
            pltpu.VMEM((groups, span, 2, rows, HEAD_SIZE), BF16),
            pltpu.VMEM((rows, 2 * rank), BF16),
            pltpu.VMEM((2, rows, cols), BF16),
            pltpu.VMEM((2, rows, rank), F32),
            pltpu.VMEM((2, rows, rank), BF16),
            pltpu.VMEM((N, rows, rank), BF16),
            pltpu.VMEM((W, rows, rank), BF16),
            pltpu.VMEM((W, 2, piece, cols), BF16),
            pltpu.VMEM((W, 2, piece, cols), BF16),
            dma((10,)),
            dma((span, 2)), dma((span, 2)),
            dma((W,)), dma((W,)),
            dma((groups, span)), dma((groups, span)),
            dma((N,)), dma((N,)),
            dma((W,)), dma((W,)),
            dma((W,)), dma((W,)),
            dma((W,)), dma((W,)),
            dma((N,)), dma((N,)),
        ],
        compiler_params=pltpu.CompilerParams(
            collective_id=0, has_side_effects=True, vmem_limit_bytes=60 * 2**20
        ),
    )(file_lengths, queries, out_grad, mem_key, memory_values, enc_rows, key_down, key_up, value_down, value_up)
    return pl.pallas_call(
        widen,
        out_shape=(
            jax.ShapeDtypeStruct((share, rank), F32),
            jax.ShapeDtypeStruct((share, rank), F32),
            jax.ShapeDtypeStruct((rank, cols), F32),
            jax.ShapeDtypeStruct((rank, cols), F32),
        ),
        in_specs=[vmem_spec] * 2,
        out_specs=(vmem_spec,) * 4,
    )(res, fin)


def solution(mesh):
    placed = (
        P(),
        P("wide", "narrow"),
        P("wide", "narrow"),
        P("wide", "narrow"),
        P("wide", "narrow"),
        P("wide", None),
        P(),
        P(None, "narrow"),
        P(),
        P(None, "narrow"),
    )

    def on_device(*args):
        W, N = lax.axis_size("wide"), lax.axis_size("narrow")
        width, rank = args[6].shape
        fits = N == 4 and width % (W * 256) == 0 and rank % (W * 16) == 0 and args[1].shape[0] % 256 == 0
        return (by_kernel if fits else by_collectives)(*args)

    return jax.shard_map(
        on_device,
        mesh=mesh,
        in_specs=placed,
        out_specs=(P("wide", None), P("wide", None), P(None, "narrow"), P(None, "narrow")),
        check_vma=False,
    )
```
